32 devices in a mesh: ch: 16 (over z, y, core), ta: 2 (over x).
Axes of the slice: x: 2, y: 2, z: 4, core: 2. Of those that a mesh axis runs over, the one named last changes fastest.
Arguments:
- templates: bfloat16 [64, 200, 8192], P('ta', None, 'ch')
- record: float32 [8192, 512], P('ch', 'ta')
- record_tail: float32 [8192, 199], P('ch')
Outputs:
- stacked: float32 [64, 512], P('ch', 'ta')
All inputs are finite; a program needn't handle non-finite values.
Results may differ from the reference program's by a relative error of at most 0.00044.
Values may be sent and summed in bfloat16 or wider, within the bound.
A program may use at most 128 MiB of HBM per device.

```python
import math
import jax
import jax.numpy as jnp
from jax import lax

C = 8192
M = 200
K = 64
LAGS = 512


def make_scene(key):
    base = jax.random.fold_in(key, 7301)
    keys = jax.random.split(base, 9)
    raw = jax.random.normal(keys[0], (K, M, C), jnp.float32)
    noise = jax.random.normal(keys[4], (C, LAGS + M - 1), jnp.float32)
    t_scale = jnp.exp(jax.random.uniform(keys[1], (K, 1, C), jnp.float32, jnp.log(0.3), jnp.log(3.0)))
    t_shift = jax.random.uniform(keys[2], (K, 1, C), jnp.float32, -1.0, 1.0)
    templ = ((raw + t_shift) * t_scale).astype(jnp.bfloat16).astype(jnp.float32)
    c_scale = jnp.exp(jax.random.uniform(keys[5], (C, 1), jnp.float32, jnp.log(0.2), jnp.log(2.0)))
    c_shift = jax.random.uniform(keys[8], (C, 1), jnp.float32, -1.0, 1.0)
    signal = noise * c_scale + c_shift
    onsets = jax.random.randint(keys[6], (K * 4,), 0, LAGS).astype(jnp.int32)
    amounts = jax.random.uniform(keys[7], (K * 4,), jnp.float32, 0.5, 2.0)

    def plant(event, current):
        which = event // 4
        piece = jnp.transpose(lax.dynamic_index_in_dim(templ, which, 0, False)) * amounts[event]
        anchor = (jnp.int32(0), onsets[event])
        present = lax.dynamic_slice(current, anchor, (C, M))
        return lax.dynamic_update_slice(current, present + piece, anchor)
    signal = lax.fori_loop(0, K * 4, plant, signal)
    return (templ.astype(jnp.bfloat16), signal)


def draw_templates(key, part):
    return make_scene(key)[0]


def draw_record(key, part):
    return make_scene(key)[1][:, :LAGS]


def draw_record_tail(key, part):
    return make_scene(key)[1][:, LAGS:]


def setup_inputs(seed: int = 0) -> dict:
    seeds = jax.random.split(jax.random.key(seed), 4)
    return {
        "templates": draw_templates(jax.random.fold_in(seeds[3], 71), 0),
        "record": draw_record(jax.random.fold_in(seeds[3], 71), 0),
        "record_tail": draw_record_tail(jax.random.fold_in(seeds[3], 71), 0),
    }


def reference(templates, record, record_tail):
    samples = templates.shape[1]
    channels = templates.shape[2]
    lag_count = record.shape[1]
    values = templates.astype(jnp.float32)
    centred = values - lax.optimization_barrier(jnp.mean(values, axis=1, keepdims=True))
    normed = (centred * lax.rsqrt(lax.optimization_barrier(jnp.mean(centred * centred, axis=1, keepdims=True)) + 1e-06) / math.sqrt(samples)).astype(jnp.bfloat16)
    full_trace = jnp.concatenate([record, record_tail], axis=1)
    block_rows = math.gcd(channels, 32)
    block_count = channels // block_rows

    def advance(running, block_index):
        first_row = (block_index * block_rows).astype(jnp.int32)
        channel_rows = lax.dynamic_slice_in_dim(full_trace, first_row, block_rows, 0)
        hankel = jnp.stack([channel_rows[:, offset:offset + lag_count] for offset in range(samples)], axis=1)
        window_mean = lax.optimization_barrier(jnp.mean(hankel, axis=1, keepdims=True))
        deviation = hankel - window_mean
        window_var = lax.optimization_barrier(jnp.mean(deviation * deviation, axis=1, keepdims=True))
        windows = (deviation * lax.rsqrt(window_var + 1e-06) / math.sqrt(samples)).astype(jnp.bfloat16)
        unit_part = lax.dynamic_slice_in_dim(normed, first_row, block_rows, 2)
        running = running + jnp.einsum('kmc,cmt->kt', unit_part.astype(jnp.float32), windows.astype(jnp.float32))
        return (running, None)
    running, unused = lax.scan(advance, jnp.zeros((templates.shape[0], lag_count), jnp.float32), jnp.arange(block_count, dtype=jnp.int32))
    return running / channels
```

```python
import functools
import math

import jax
import jax.numpy as jnp
from jax import lax
from jax.experimental import pallas as pl
from jax.experimental.pallas import tpu as pltpu
from jax.sharding import PartitionSpec as P

LANES = 128
SHIFTS = 8
VMEM_LIMIT = 56 * 1024 * 1024


def normalize_kernel(t_ref, u_ref, wide):
    rows, samples, _ = t_ref.shape

    def one(k, carry):
        values = t_ref[k].astype(jnp.float32)
        centred = values - jnp.mean(values, axis=0, keepdims=True)
        power = jnp.mean(centred * centred, axis=0, keepdims=True)
        wide[pl.ds(k, samples, stride=rows), :] = centred * (
            lax.rsqrt(power + 1e-06) * (1.0 / math.sqrt(samples))
        )
        return carry

    lax.fori_loop(0, rows, one, 0)

    def cast(m, carry):
        u_ref[0, m] = wide[pl.ds(pl.multiple_of(m * rows, rows), rows), :].astype(jnp.bfloat16)
        return carry

    lax.fori_loop(0, samples, cast, 0)


def normalize(templates, tile):
    count, samples, channels = templates.shape
    rows = math.gcd(count, 16)
    per_tile = tile // LANES
    return pl.pallas_call(
        normalize_kernel,
        grid=(channels // tile, per_tile, count // rows),
        in_specs=[pl.BlockSpec((rows, samples, LANES), lambda i, h, r: (r, 0, i * per_tile + h))],
        out_specs=pl.BlockSpec((1, samples, rows, LANES), lambda i, h, r: (i, 0, r, h)),
        out_shape=jax.ShapeDtypeStruct((channels // tile, samples, count, tile), jnp.bfloat16),
        scratch_shapes=[pltpu.VMEM((samples * rows, LANES), jnp.float32)],
        compiler_params=pltpu.CompilerParams(vmem_limit_bytes=VMEM_LIMIT),
        name="normalize_templates",
    )(templates)


def merge(left, right, n_left, n_right):
    (a0, v0), (a1, v1) = left, right
    w1 = n_right / (n_left + n_right)
    w0 = 1.0 - w1
    gap = a1 - a0
    return (a0 + w1 * gap, w0 * v0 + w1 * v1 + (w0 * w1) * (gap * gap))


def window_stats(x, samples, lag_count):
    mean, var, length = x, jnp.zeros_like(x), 1
    total, done = None, 0
    while True:
        if samples & length:
            piece = (mean[done : done + lag_count], var[done : done + lag_count])
            total = piece if total is None else merge(total, piece, done, length)
            done += length
        if 2 * length > samples:
            return total
        keep = mean.shape[0] - length
        mean, var = merge(
            (mean[:keep], var[:keep]), (mean[length:], var[length:]), length, length
        )
        length *= 2


def correlate_kernel(steps, groups, blocks, x_ref, u_ref, out_ref, xs, mu, rs, w_even, w_odd, acc):
    step = pl.program_id(0)
    rows = w_even.shape[0]
    tile = x_ref.shape[1]
    lag_count = mu.shape[0]
    samples = groups * SHIFTS
    reach = xs.shape[1]
    now = jnp.minimum(step, steps - 1)
    before = jnp.maximum(step - 1, 0)
    block_now = lax.rem(now // groups, blocks)
    block_before = lax.rem(before // groups, blocks)
    first_row = pl.multiple_of(block_now * rows, rows)
    x_row = first_row + lax.rem(now, groups) * SHIFTS

    @pl.when(step == 0)
    def _():
        acc[...] = jnp.zeros_like(acc)
        w_odd[...] = jnp.zeros_like(w_odd)

    @pl.when(lax.rem(step, groups * blocks) == 0)
    def _():
        x = x_ref[...]
        mean, var = window_stats(x, samples, lag_count)
        mu[...] = mean
        rs[...] = lax.rsqrt(var + 1e-06) * (1.0 / math.sqrt(samples))
        for j in range(SHIFTS):
            xs[j] = x[j : j + reach]

    def work(w_now, w_before):
        chunk = math.gcd(rows, 32)
        weights = jnp.concatenate([u_ref[0, j] for j in range(SHIFTS)], axis=1)
        acc_rows = pl.ds(pl.multiple_of(block_before * rows, rows), rows)
        acc[acc_rows, :] += lax.dot_general(
            w_before[...], weights, (((1,), (1,)), ((), ())), preferred_element_type=jnp.float32
        )
        for r in range(0, rows, chunk):
            mean = mu[pl.ds(first_row + r, chunk), :]
            scale = rs[pl.ds(first_row + r, chunk), :]
            for j in range(SHIFTS):
                values = xs[j, pl.ds(pl.multiple_of(x_row + r, 8), chunk), :]
                w_now[pl.ds(r, chunk), pl.ds(j * tile, tile)] = (
                    (values - mean) * scale
                ).astype(jnp.bfloat16)

    @pl.when(lax.rem(step, 2) == 0)
    def _():
        work(w_even, w_odd)

    @pl.when(lax.rem(step, 2) == 1)
    def _():
        work(w_odd, w_even)

    @pl.when(step == steps)
    def _():
        out_ref[...] = acc[...]


def correlate(unit, trace, lag_count):
    tiles, samples, count, tile = unit.shape
    span = trace.shape[0]
    groups = samples // SHIFTS
    rows = math.gcd(lag_count, 512)
    blocks = lag_count // rows
    steps = tiles * blocks * groups
    per_tile = blocks * groups
    reach = lag_count + samples - SHIFTS
    return pl.pallas_call(
        functools.partial(correlate_kernel, steps, groups, blocks),
        grid=(steps + 1,),
        in_specs=[
            pl.BlockSpec((span, tile), lambda s: (0, jnp.minimum(s, steps - 1) // per_tile)),
            pl.BlockSpec(
                (1, SHIFTS, count, tile),
                lambda s: (
                    jnp.maximum(s - 1, 0) // per_tile,
                    lax.rem(jnp.maximum(s - 1, 0), groups),
                    0,
                    0,
                ),
            ),
        ],
        out_specs=pl.BlockSpec((lag_count, count), lambda s: (0, 0)),
        out_shape=jax.ShapeDtypeStruct((lag_count, count), jnp.float32),
        scratch_shapes=[
            pltpu.VMEM((SHIFTS, reach, tile), jnp.float32),
            pltpu.VMEM((lag_count, tile), jnp.float32),
            pltpu.VMEM((lag_count, tile), jnp.float32),
            pltpu.VMEM((rows, SHIFTS * tile), jnp.bfloat16),
            pltpu.VMEM((rows, SHIFTS * tile), jnp.bfloat16),
            pltpu.VMEM((lag_count, count), jnp.float32),
        ],
        compiler_params=pltpu.CompilerParams(vmem_limit_bytes=VMEM_LIMIT),
        name="correlate_windows",
    )(trace, unit)


def on_device(templates, record, record_tail):
    n_chan = lax.axis_size("ch")
    n_time = lax.axis_size("ta")
    tile = math.gcd(record.shape[0], 2 * LANES)
    unit = normalize(templates, tile)
    own = jnp.transpose(record)
    full_time = lax.all_gather(own, "ta", axis=0, tiled=True)
    trace = jnp.concatenate([full_time, jnp.transpose(record_tail)], axis=0)
    lag_count = full_time.shape[0]
    partial_value = jnp.transpose(correlate(unit, trace, lag_count))
    here = partial_value.shape[0]
    count_all = here * n_time
    lag_dev = lag_count // n_time
    placed = lax.dynamic_update_slice(
        jnp.zeros((count_all, lag_count), jnp.float32),
        partial_value,
        (lax.axis_index("ta") * here, 0),
    )
    arranged = (
        placed.reshape(n_chan, count_all // n_chan, n_time, lag_dev)
        .transpose(0, 2, 1, 3)
        .reshape(n_chan * n_time, count_all // n_chan, lag_dev)
    )
    stacked = lax.psum_scatter(arranged, ("ch", "ta"), scatter_dimension=0, tiled=True)[0]
    return stacked * (1.0 / (n_chan * record.shape[0]))


def solution(mesh):
    return jax.shard_map(
        on_device,
        mesh=mesh,
        in_specs=(P("ta", None, "ch"), P("ch", "ta"), P("ch", None)),
        out_specs=P("ch", "ta"),
        check_vma=False,
    )
```

```python
import functools
import math

import jax
import jax.numpy as jnp
from jax import lax
from jax.experimental import pallas as pl
from jax.experimental.pallas import tpu as pltpu
from jax.sharding import PartitionSpec as P

LANES = 128
SHIFTS = 8
VMEM_LIMIT = 56 * 1024 * 1024


def normalize_kernel(t_ref, u_ref, wide):
    rows, samples, _ = t_ref.shape

    def one(k, carry):
        values = t_ref[k].astype(jnp.float32)
        centred = values - jnp.mean(values, axis=0, keepdims=True)
        power = jnp.mean(centred * centred, axis=0, keepdims=True)
        wide[pl.ds(k, samples, stride=rows), :] = centred * (
            lax.rsqrt(power + 1e-06) * (1.0 / math.sqrt(samples))
        )
        return carry

    lax.fori_loop(0, rows, one, 0, unroll=4)

    def cast(i, carry):
        first = i * SHIFTS
        part = wide[pl.ds(pl.multiple_of(first * rows, 8), SHIFTS * rows), :]
        u_ref[0, pl.ds(first, SHIFTS)] = part.reshape(SHIFTS, rows, LANES).astype(jnp.bfloat16)
        return carry

    lax.fori_loop(0, samples // SHIFTS, cast, 0, unroll=5)


def normalize(templates, tile):
    count, samples, channels = templates.shape
    rows = math.gcd(count, 16)
    per_tile = tile // LANES
    return pl.pallas_call(
        normalize_kernel,
        grid=(channels // tile, per_tile, count // rows),
        in_specs=[pl.BlockSpec((rows, samples, LANES), lambda i, h, r: (r, 0, i * per_tile + h))],
        out_specs=pl.BlockSpec((1, samples, rows, LANES), lambda i, h, r: (i, 0, r, h)),
        out_shape=jax.ShapeDtypeStruct((channels // tile, samples, count, tile), jnp.bfloat16),
        scratch_shapes=[pltpu.VMEM((samples * rows, LANES), jnp.float32)],
        compiler_params=pltpu.CompilerParams(vmem_limit_bytes=VMEM_LIMIT),
        name="normalize_templates",
    )(templates)


def merge(left, right, n_left, n_right):
    (a0, v0), (a1, v1) = left, right
    w1 = n_right / (n_left + n_right)
    w0 = 1.0 - w1
    gap = a1 - a0
    return (a0 + w1 * gap, w0 * v0 + w1 * v1 + (w0 * w1) * (gap * gap))


def window_stats(x, samples, lag_count):
    mean, var, length = x, jnp.zeros_like(x), 1
    total, done = None, 0
    while True:
        if samples & length:
            piece = (mean[done : done + lag_count], var[done : done + lag_count])
            total = piece if total is None else merge(total, piece, done, length)
            done += length
        if 2 * length > samples:
            return total
        keep = mean.shape[0] - length
        mean, var = merge(
            (mean[:keep], var[:keep]), (mean[length:], var[length:]), length, length
        )
        length *= 2


def correlate_kernel(steps, groups, blocks, x_ref, u_ref, out_ref, xs, mu, rs, w_even, w_odd, acc):
    step = pl.program_id(0)
    rows = w_even.shape[0]
    tile = x_ref.shape[1]
    lag_count = mu.shape[0]
    samples = groups * SHIFTS
    reach = xs.shape[1]
    now = jnp.minimum(step, steps - 1)
    before = jnp.maximum(step - 1, 0)
    block_now = lax.rem(now // groups, blocks)
    block_before = lax.rem(before // groups, blocks)
    first_row = pl.multiple_of(block_now * rows, rows)
    x_row = first_row + lax.rem(now, groups) * SHIFTS

    @pl.when(step == 0)
    def _():
        acc[...] = jnp.zeros_like(acc)
        w_odd[...] = jnp.zeros_like(w_odd)

    @pl.when(lax.rem(step, groups * blocks) == 0)
    def _():
        x = x_ref[...]
        mean, var = window_stats(x, samples, lag_count)
        mu[...] = mean
        rs[...] = lax.rsqrt(var + 1e-06) * (1.0 / math.sqrt(samples))
        for j in range(SHIFTS):
            xs[j] = x[j : j + reach]

    def work(w_now, w_before):
        chunk = math.gcd(rows, 32)
        weights = jnp.concatenate([u_ref[0, j] for j in range(SHIFTS)], axis=1)
        acc_lags = pl.ds(pl.multiple_of(block_before * rows, rows), rows)
        acc[:, acc_lags] += lax.dot_general(
            weights, w_before[...], (((1,), (1,)), ((), ())), preferred_element_type=jnp.float32
        )
        for r in range(0, rows, chunk):
            mean = mu[pl.ds(first_row + r, chunk), :]
            scale = rs[pl.ds(first_row + r, chunk), :]
            for j in range(SHIFTS):
                values = xs[j, pl.ds(pl.multiple_of(x_row + r, 8), chunk), :]
                w_now[pl.ds(r, chunk), pl.ds(j * tile, tile)] = (
                    (values - mean) * scale
                ).astype(jnp.bfloat16)

    @pl.when(lax.rem(step, 2) == 0)
    def _():
        work(w_even, w_odd)

    @pl.when(lax.rem(step, 2) == 1)
    def _():
        work(w_odd, w_even)

    @pl.when(step == steps)
    def _():
        out_ref[...] = acc[...]


def correlate(unit, trace, lag_count):
    tiles, samples, count, tile = unit.shape
    span = trace.shape[0]
    groups = samples // SHIFTS
    rows = math.gcd(lag_count, 512)
    blocks = lag_count // rows
    steps = tiles * blocks * groups
    per_tile = blocks * groups
    reach = lag_count + samples - SHIFTS
    return pl.pallas_call(
        functools.partial(correlate_kernel, steps, groups, blocks),
        grid=(steps + 1,),
        in_specs=[
            pl.BlockSpec((span, tile), lambda s: (0, jnp.minimum(s, steps - 1) // per_tile)),
            pl.BlockSpec(
                (1, SHIFTS, count, tile),
                lambda s: (
                    jnp.maximum(s - 1, 0) // per_tile,
                    lax.rem(jnp.maximum(s - 1, 0), groups),
                    0,
                    0,
                ),
            ),
        ],
        out_specs=pl.BlockSpec((count, lag_count), lambda s: (0, 0)),
        out_shape=jax.ShapeDtypeStruct((count, lag_count), jnp.float32),
        scratch_shapes=[
            pltpu.VMEM((SHIFTS, reach, tile), jnp.float32),
            pltpu.VMEM((lag_count, tile), jnp.float32),
            pltpu.VMEM((lag_count, tile), jnp.float32),
            pltpu.VMEM((rows, SHIFTS * tile), jnp.bfloat16),
            pltpu.VMEM((rows, SHIFTS * tile), jnp.bfloat16),
            pltpu.VMEM((count, lag_count), jnp.float32),
        ],
        compiler_params=pltpu.CompilerParams(vmem_limit_bytes=VMEM_LIMIT),
        name="correlate_windows",
    )(trace, unit)


def sum_kernel(scale, part_ref, out_ref, outgoing, arrived, send_sem, recv_sem):
    n_chan, n_time = lax.axis_size("ch"), lax.axis_size("ta")
    chan, time = lax.axis_index("ch"), lax.axis_index("ta")
    owners = n_chan // n_time
    block, lags = out_ref.shape
    giver = chan // owners
    own = giver == time

    barrier = pltpu.get_barrier_semaphore()
    for i in range(n_chan):

        @pl.when(jnp.logical_not(own & (chan == i)))
        def _():
            pl.semaphore_signal(
                barrier, inc=1, device_id=(i, giver), device_id_type=pl.DeviceIdType.MESH
            )

    for r in range(owners):
        for b in range(n_time):
            outgoing[r * n_time + b] = part_ref[
                pl.ds(r * block, block), pl.ds(b * lags, lags)
            ]
    pl.semaphore_wait(barrier, owners * n_time - own.astype(jnp.int32))

    def copy(slot, r, b):
        return pltpu.make_async_remote_copy(
            src_ref=outgoing.at[slot],
            dst_ref=arrived.at[chan],
            send_sem=send_sem.at[slot],
            recv_sem=recv_sem.at[chan],
            device_id=(time * owners + r, b),
            device_id_type=pl.DeviceIdType.MESH,
        )

    for r in range(owners):
        for b in range(n_time):
            slot = r * n_time + b
            mine = (time * owners + r == chan) & (time == b)

            @pl.when(jnp.logical_not(mine))
            def _():
                copy(slot, r, b).start()

            @pl.when(mine)
            def _():
                arrived[chan] = outgoing[slot]

    for i in range(n_chan):

        @pl.when(jnp.logical_not(own & (chan == i)))
        def _():
            pltpu.make_async_remote_copy(
                src_ref=outgoing.at[0],
                dst_ref=arrived.at[i],
                send_sem=send_sem.at[0],
                recv_sem=recv_sem.at[i],
                device_id=(i, giver),
                device_id_type=pl.DeviceIdType.MESH,
            ).wait_recv()

    total = arrived[0]
    for i in range(1, n_chan):
        total = total + arrived[i]
    out_ref[...] = total * scale

    for r in range(owners):
        for b in range(n_time):
            mine = (time * owners + r == chan) & (time == b)

            @pl.when(jnp.logical_not(mine))
            def _():
                copy(r * n_time + b, r, b).wait_send()


def sum_to_owners(part, n_chan, n_time, scale):
    count, lag_count = part.shape
    owners = n_chan // n_time
    block, lags = count // owners, lag_count // n_time
    return pl.pallas_call(
        functools.partial(sum_kernel, scale),
        out_shape=jax.ShapeDtypeStruct((block, lags), jnp.float32),
        in_specs=[pl.BlockSpec(memory_space=pltpu.VMEM)],
        out_specs=pl.BlockSpec(memory_space=pltpu.VMEM),
        scratch_shapes=[
            pltpu.VMEM((owners * n_time, block, lags), jnp.float32),
            pltpu.VMEM((n_chan, block, lags), jnp.float32),
            pltpu.SemaphoreType.DMA((owners * n_time,)),
            pltpu.SemaphoreType.DMA((n_chan,)),
        ],
        compiler_params=pltpu.CompilerParams(
            collective_id=0, has_side_effects=True, vmem_limit_bytes=VMEM_LIMIT
        ),
        name="sum_to_owners",
    )(part)


def on_device(templates, record, record_tail):
    n_chan = lax.axis_size("ch")
    n_time = lax.axis_size("ta")
    tile = math.gcd(record.shape[0], 2 * LANES)
    unit = normalize(templates, tile)
    own = jnp.transpose(record)
    full_time = lax.all_gather(own, "ta", axis=0, tiled=True)
    trace = jnp.concatenate([full_time, jnp.transpose(record_tail)], axis=0)
    part = correlate(unit, trace, full_time.shape[0])
    return sum_to_owners(part, n_chan, n_time, 1.0 / (n_chan * record.shape[0]))


def solution(mesh):
    return jax.shard_map(
        on_device,
        mesh=mesh,
        in_specs=(P("ta", None, "ch"), P("ch", "ta"), P("ch", None)),
        out_specs=P("ch", "ta"),
        check_vma=False,
    )
```

```python
import functools
import math

import jax
import jax.numpy as jnp
from jax import lax
from jax.experimental import pallas as pl
from jax.experimental.pallas import tpu as pltpu
from jax.sharding import PartitionSpec as P

LANES = 128
SHIFTS = 8
VMEM_LIMIT = 56 * 1024 * 1024


def prepare_kernel(last, t_ref, rec_ref, tail_ref, u_ref, trace_ref, wide, slabs, send_sem, recv_sem):
    n_time = lax.axis_size("ta")
    time = lax.axis_index("ta")
    rows, samples, _ = t_ref.shape
    lags = rec_ref.shape[1]
    step = (pl.program_id(0) * pl.num_programs(1) + pl.program_id(1)) * pl.num_programs(
        2
    ) + pl.program_id(2)

    def copy(i):
        return pltpu.make_async_remote_copy(
            src_ref=slabs.at[time],
            dst_ref=slabs.at[time],
            send_sem=send_sem.at[i - 1],
            recv_sem=recv_sem.at[i - 1],
            device_id={"ta": lax.rem(time + i, n_time)},
            device_id_type=pl.DeviceIdType.MESH,
        )

    @pl.when(step == 0)
    def _():
        barrier = pltpu.get_barrier_semaphore()
        for i in range(1, n_time):
            pl.semaphore_signal(
                barrier,
                inc=1,
                device_id={"ta": lax.rem(time + i, n_time)},
                device_id_type=pl.DeviceIdType.MESH,
            )
        slabs[time] = jnp.transpose(rec_ref[...])
        pl.semaphore_wait(barrier, n_time - 1)
        for i in range(1, n_time):
            copy(i).start()

    def one(k, carry):
        values = t_ref[k].astype(jnp.float32)
        centred = values - jnp.mean(values, axis=0, keepdims=True)
        power = jnp.mean(centred * centred, axis=0, keepdims=True)
        wide[pl.ds(k, samples, stride=rows), :] = centred * (
            lax.rsqrt(power + 1e-06) * (1.0 / math.sqrt(samples))
        )
        return carry

    lax.fori_loop(0, rows, one, 0, unroll=4)

    def cast(i, carry):
        first = i * SHIFTS
        part = wide[pl.ds(pl.multiple_of(first * rows, 8), SHIFTS * rows), :]
        u_ref[0, pl.ds(first, SHIFTS)] = part.reshape(SHIFTS, rows, LANES).astype(jnp.bfloat16)
        return carry

    lax.fori_loop(0, samples // SHIFTS, cast, 0, unroll=5)

    @pl.when(step == last)
    def _():
        trace_ref[pl.ds(n_time * lags, tail_ref.shape[0]), :] = tail_ref[...]
        for i in range(1, n_time):
            copy(i).wait_recv()
        for i in range(n_time):
            trace_ref[pl.ds(i * lags, lags), :] = slabs[i]
        for i in range(1, n_time):
            copy(i).wait_send()


def prepare(templates, record, tail, n_time, tile):
    count, samples, channels = templates.shape
    lags = record.shape[1]
    span = n_time * lags + tail.shape[0]
    rows = math.gcd(count, 16)
    per_tile = tile // LANES
    grid = (channels // tile, per_tile, count // rows)
    return pl.pallas_call(
        functools.partial(prepare_kernel, math.prod(grid) - 1),
        grid=grid,
        in_specs=[
            pl.BlockSpec((rows, samples, LANES), lambda i, h, r: (r, 0, i * per_tile + h)),
            pl.BlockSpec(record.shape, lambda i, h, r: (0, 0)),
            pl.BlockSpec(tail.shape, lambda i, h, r: (0, 0)),
        ],
        out_specs=[
            pl.BlockSpec((1, samples, rows, LANES), lambda i, h, r: (i, 0, r, h)),
            pl.BlockSpec((span, channels), lambda i, h, r: (0, 0)),
        ],
        out_shape=[
            jax.ShapeDtypeStruct((channels // tile, samples, count, tile), jnp.bfloat16),
            jax.ShapeDtypeStruct((span, channels), jnp.float32),
        ],
        scratch_shapes=[
            pltpu.VMEM((samples * rows, LANES), jnp.float32),
            pltpu.VMEM((n_time, lags, channels), jnp.float32),
            pltpu.SemaphoreType.DMA((n_time - 1,)),
            pltpu.SemaphoreType.DMA((n_time - 1,)),
        ],
        compiler_params=pltpu.CompilerParams(
            collective_id=1, has_side_effects=True, vmem_limit_bytes=VMEM_LIMIT
        ),
        name="prepare",
    )(templates, record, tail)


def merge(left, right, n_left, n_right):
    (a0, v0), (a1, v1) = left, right
    w1 = n_right / (n_left + n_right)
    w0 = 1.0 - w1
    gap = a1 - a0
    return (a0 + w1 * gap, w0 * v0 + w1 * v1 + (w0 * w1) * (gap * gap))


def window_stats(x, samples, lag_count):
    mean, var, length = x, jnp.zeros_like(x), 1
    total, done = None, 0
    while True:
        if samples & length:
            piece = (mean[done : done + lag_count], var[done : done + lag_count])
            total = piece if total is None else merge(total, piece, done, length)
            done += length
        if 2 * length > samples:
            return total
        keep = mean.shape[0] - length
        mean, var = merge(
            (mean[:keep], var[:keep]), (mean[length:], var[length:]), length, length
        )
        length *= 2


def correlate_kernel(groups, blocks, x_ref, u_ref, out_ref, xs, mu, rs, w_even, w_odd):
    rows = w_even.shape[0]
    tile = x_ref.shape[1]
    lag_count = mu.shape[0]
    samples = groups * SHIFTS
    reach = xs.shape[1]
    steps = groups * blocks

    @pl.when(pl.program_id(0) == 0)
    def _():
        out_ref[...] = jnp.zeros_like(out_ref)

    x = x_ref[...]
    mean, var = window_stats(x, samples, lag_count)
    mu[...] = mean
    rs[...] = lax.rsqrt(var + 1e-06) * (1.0 / math.sqrt(samples))
    for j in range(SHIFTS):
        xs[j] = x[j : j + reach]

    def build(step, w):
        first_row = pl.multiple_of((step // groups) * rows, rows)
        x_row = first_row + lax.rem(step, groups) * SHIFTS
        chunk = math.gcd(rows, 32)
        for r in range(0, rows, chunk):
            mean = mu[pl.ds(first_row + r, chunk), :]
            scale = rs[pl.ds(first_row + r, chunk), :]
            for j in range(SHIFTS):
                values = xs[j, pl.ds(pl.multiple_of(x_row + r, 8), chunk), :]
                w[pl.ds(r, chunk), pl.ds(j * tile, tile)] = ((values - mean) * scale).astype(
                    jnp.bfloat16
                )

    def multiply(step, w):
        first_row = pl.multiple_of((step // groups) * rows, rows)
        first = lax.rem(step, groups) * SHIFTS
        weights = jnp.concatenate([u_ref[0, first + j] for j in range(SHIFTS)], axis=1)
        out_ref[:, pl.ds(first_row, rows)] += lax.dot_general(
            weights, w[...], (((1,), (1,)), ((), ())), preferred_element_type=jnp.float32
        )

    build(jnp.int32(0), w_even)

    def pair(i, carry):
        multiply(2 * i, w_even)
        build(2 * i + 1, w_odd)
        multiply(2 * i + 1, w_odd)
        build(2 * i + 2, w_even)
        return carry

    pairs = (steps - 1) // 2
    lax.fori_loop(0, pairs, pair, 0)
    multiply(jnp.int32(2 * pairs), w_even)
    if 2 * pairs + 1 < steps:
        build(jnp.int32(steps - 1), w_odd)
        multiply(jnp.int32(steps - 1), w_odd)


def correlate(unit, trace, lag_count):
    tiles, samples, count, tile = unit.shape
    span = trace.shape[0]
    groups = samples // SHIFTS
    rows = math.gcd(lag_count, 512)
    reach = lag_count + samples - SHIFTS
    return pl.pallas_call(
        functools.partial(correlate_kernel, groups, lag_count // rows),
        grid=(tiles,),
        in_specs=[
            pl.BlockSpec((span, tile), lambda i: (0, i)),
            pl.BlockSpec((1, samples, count, tile), lambda i: (i, 0, 0, 0)),
        ],
        out_specs=pl.BlockSpec((count, lag_count), lambda i: (0, 0)),
        out_shape=jax.ShapeDtypeStruct((count, lag_count), jnp.float32),
        scratch_shapes=[
            pltpu.VMEM((SHIFTS, reach, tile), jnp.float32),
            pltpu.VMEM((lag_count, tile), jnp.float32),
            pltpu.VMEM((lag_count, tile), jnp.float32),
            pltpu.VMEM((rows, SHIFTS * tile), jnp.bfloat16),
            pltpu.VMEM((rows, SHIFTS * tile), jnp.bfloat16),
        ],
        compiler_params=pltpu.CompilerParams(vmem_limit_bytes=VMEM_LIMIT),
        name="correlate_windows",
    )(trace, unit)


def sum_kernel(scale, part_ref, out_ref, outgoing, arrived, send_sem, recv_sem):
    n_chan, n_time = lax.axis_size("ch"), lax.axis_size("ta")
    chan, time = lax.axis_index("ch"), lax.axis_index("ta")
    owners = n_chan // n_time
    block, lags = out_ref.shape
    giver = chan // owners
    own = giver == time

    barrier = pltpu.get_barrier_semaphore()
    for i in range(n_chan):

        @pl.when(jnp.logical_not(own & (chan == i)))
        def _():
            pl.semaphore_signal(
                barrier, inc=1, device_id=(i, giver), device_id_type=pl.DeviceIdType.MESH
            )

    for r in range(owners):
        for b in range(n_time):
            outgoing[r * n_time + b] = part_ref[
                pl.ds(r * block, block), pl.ds(b * lags, lags)
            ]
    pl.semaphore_wait(barrier, owners * n_time - own.astype(jnp.int32))

    def copy(slot, r, b):
        return pltpu.make_async_remote_copy(
            src_ref=outgoing.at[slot],
            dst_ref=arrived.at[chan],
            send_sem=send_sem.at[slot],
            recv_sem=recv_sem.at[chan],
            device_id=(time * owners + r, b),
            device_id_type=pl.DeviceIdType.MESH,
        )

    for r in range(owners):
        for b in range(n_time):
            slot = r * n_time + b
            mine = (time * owners + r == chan) & (time == b)

            @pl.when(jnp.logical_not(mine))
            def _():
                copy(slot, r, b).start()

            @pl.when(mine)
            def _():
                arrived[chan] = outgoing[slot]

    for i in range(n_chan):

        @pl.when(jnp.logical_not(own & (chan == i)))
        def _():
            pltpu.make_async_remote_copy(
                src_ref=outgoing.at[0],
                dst_ref=arrived.at[i],
                send_sem=send_sem.at[0],
                recv_sem=recv_sem.at[i],
                device_id=(i, giver),
                device_id_type=pl.DeviceIdType.MESH,
            ).wait_recv()

    total = arrived[0]
    for i in range(1, n_chan):
        total = total + arrived[i]
    out_ref[...] = total * scale

    for r in range(owners):
        for b in range(n_time):
            mine = (time * owners + r == chan) & (time == b)

            @pl.when(jnp.logical_not(mine))
            def _():
                copy(r * n_time + b, r, b).wait_send()


def sum_to_owners(part, n_chan, n_time, scale):
    count, lag_count = part.shape
    owners = n_chan // n_time
    block, lags = count // owners, lag_count // n_time
    return pl.pallas_call(
        functools.partial(sum_kernel, scale),
        out_shape=jax.ShapeDtypeStruct((block, lags), jnp.float32),
        in_specs=[pl.BlockSpec(memory_space=pltpu.VMEM)],
        out_specs=pl.BlockSpec(memory_space=pltpu.VMEM),
        scratch_shapes=[
            pltpu.VMEM((owners * n_time, block, lags), jnp.float32),
            pltpu.VMEM((n_chan, block, lags), jnp.float32),
            pltpu.SemaphoreType.DMA((owners * n_time,)),
            pltpu.SemaphoreType.DMA((n_chan,)),
        ],
        compiler_params=pltpu.CompilerParams(
            collective_id=0, has_side_effects=True, vmem_limit_bytes=VMEM_LIMIT
        ),
        name="sum_to_owners",
    )(part)


def on_device(templates, record, record_tail):
    n_chan = lax.axis_size("ch")
    n_time = lax.axis_size("ta")
    tile = math.gcd(record.shape[0], 2 * LANES)
    unit, trace = prepare(templates, record, jnp.transpose(record_tail), n_time, tile)
    part = correlate(unit, trace, record.shape[1] * n_time)
    return sum_to_owners(part, n_chan, n_time, 1.0 / (n_chan * record.shape[0]))


def solution(mesh):
    return jax.shard_map(
        on_device,
        mesh=mesh,
        in_specs=(P("ta", None, "ch"), P("ch", "ta"), P("ch", None)),
        out_specs=P("ch", "ta"),
        check_vma=False,
    )
```

```python
import functools
import math

import jax
import jax.numpy as jnp
from jax import lax
from jax.experimental import pallas as pl
from jax.experimental.pallas import tpu as pltpu
from jax.sharding import PartitionSpec as P

LANES = 128
SHIFTS = 8
VMEM_LIMIT = 56 * 1024 * 1024


def prepare_kernel(last, t_ref, rec_ref, tail_ref, u_ref, trace_ref, wide, slabs, send_sem, recv_sem):
    n_time = lax.axis_size("ta")
    time = lax.axis_index("ta")
    rows, samples, _ = t_ref.shape
    lags = rec_ref.shape[1]
    step = (pl.program_id(0) * pl.num_programs(1) + pl.program_id(1)) * pl.num_programs(
        2
    ) + pl.program_id(2)

    def copy(i):
        return pltpu.make_async_remote_copy(
            src_ref=slabs.at[time],
            dst_ref=slabs.at[time],
            send_sem=send_sem.at[i - 1],
            recv_sem=recv_sem.at[i - 1],
            device_id={"ta": lax.rem(time + i, n_time)},
            device_id_type=pl.DeviceIdType.MESH,
        )

    @pl.when(step == 0)
    def _():
        barrier = pltpu.get_barrier_semaphore()
        for i in range(1, n_time):
            pl.semaphore_signal(
                barrier,
                inc=1,
                device_id={"ta": lax.rem(time + i, n_time)},
                device_id_type=pl.DeviceIdType.MESH,
            )
        slabs[time] = jnp.transpose(rec_ref[...])
        pl.semaphore_wait(barrier, n_time - 1)
        for i in range(1, n_time):
            copy(i).start()

    def one(k, carry):
        values = t_ref[k].astype(jnp.float32)
        centred = values - jnp.mean(values, axis=0, keepdims=True)
        power = jnp.mean(centred * centred, axis=0, keepdims=True)
        wide[pl.ds(k, samples, stride=rows), :] = centred * (
            lax.rsqrt(power + 1e-06) * (1.0 / math.sqrt(samples))
        )
        return carry

    lax.fori_loop(0, rows, one, 0, unroll=4)

    def cast(i, carry):
        first = i * SHIFTS
        part = wide[pl.ds(pl.multiple_of(first * rows, 8), SHIFTS * rows), :]
        u_ref[0, pl.ds(first, SHIFTS)] = part.reshape(SHIFTS, rows, LANES).astype(jnp.bfloat16)
        return carry

    lax.fori_loop(0, samples // SHIFTS, cast, 0, unroll=5)

    @pl.when(step == last)
    def _():
        trace_ref[pl.ds(n_time * lags, tail_ref.shape[0]), :] = tail_ref[...]
        for i in range(1, n_time):
            copy(i).wait_recv()
        for i in range(n_time):
            trace_ref[pl.ds(i * lags, lags), :] = slabs[i]
        for i in range(1, n_time):
            copy(i).wait_send()


def prepare(templates, record, tail, n_time, tile):
    count, samples, channels = templates.shape
    lags = record.shape[1]
    span = n_time * lags + tail.shape[0]
    rows = math.gcd(count, 16)
    per_tile = tile // LANES
    grid = (channels // tile, per_tile, count // rows)
    return pl.pallas_call(
        functools.partial(prepare_kernel, math.prod(grid) - 1),
        grid=grid,
        in_specs=[
            pl.BlockSpec((rows, samples, LANES), lambda i, h, r: (r, 0, i * per_tile + h)),
            pl.BlockSpec(record.shape, lambda i, h, r: (0, 0)),
            pl.BlockSpec(tail.shape, lambda i, h, r: (0, 0)),
        ],
        out_specs=[
            pl.BlockSpec((1, samples, rows, LANES), lambda i, h, r: (i, 0, r, h)),
            pl.BlockSpec((span, channels), lambda i, h, r: (0, 0)),
        ],
        out_shape=[
            jax.ShapeDtypeStruct((channels // tile, samples, count, tile), jnp.bfloat16),
            jax.ShapeDtypeStruct((span, channels), jnp.float32),
        ],
        scratch_shapes=[
            pltpu.VMEM((samples * rows, LANES), jnp.float32),
            pltpu.VMEM((n_time, lags, channels), jnp.float32),
            pltpu.SemaphoreType.DMA((n_time - 1,)),
            pltpu.SemaphoreType.DMA((n_time - 1,)),
        ],
        compiler_params=pltpu.CompilerParams(
            collective_id=1, has_side_effects=True, vmem_limit_bytes=VMEM_LIMIT
        ),
        name="prepare",
    )(templates, record, tail)


def merge(left, right, n_left, n_right):
    (a0, v0), (a1, v1) = left, right
    w1 = n_right / (n_left + n_right)
    w0 = 1.0 - w1
    gap = a1 - a0
    return (a0 + w1 * gap, w0 * v0 + w1 * v1 + (w0 * w1) * (gap * gap))


def window_stats(x, samples, lag_count):
    mean, var, length = x, jnp.zeros_like(x), 1
    total, done = None, 0
    while True:
        if samples & length:
            piece = (mean[done : done + lag_count], var[done : done + lag_count])
            total = piece if total is None else merge(total, piece, done, length)
            done += length
        if 2 * length > samples:
            return total
        keep = mean.shape[0] - length
        mean, var = merge(
            (mean[:keep], var[:keep]), (mean[length:], var[length:]), length, length
        )
        length *= 2


def correlate_kernel(groups, blocks, x_ref, u_ref, out_ref, xs, mu, rs, w_even, w_odd, early):
    rows = w_even.shape[0]
    tile = x_ref.shape[1]
    lag_count = mu.shape[0]
    samples = groups * SHIFTS
    reach = xs.shape[1]
    steps = groups * blocks

    @pl.when(pl.program_id(0) == 0)
    def _():
        out_ref[...] = jnp.zeros_like(out_ref)
        early[...] = jnp.zeros_like(early)

    x = x_ref[...]
    mean, var = window_stats(x, samples, lag_count)
    mu[...] = mean
    rs[...] = lax.rsqrt(var + 1e-06) * (1.0 / math.sqrt(samples))
    for j in range(SHIFTS):
        xs[j] = x[j : j + reach]

    half = rows // 2
    chunk = math.gcd(rows, 32)
    slices = math.gcd(4, rows // chunk)
    per_slice = SHIFTS // slices

    def build(step, w, part):
        first_row = pl.multiple_of((step // groups) * rows, rows)
        x_row = first_row + lax.rem(step, groups) * SHIFTS
        for r in range(part * (rows // slices), (part + 1) * (rows // slices), chunk):
            mean = mu[pl.ds(first_row + r, chunk), :]
            scale = rs[pl.ds(first_row + r, chunk), :]
            for j in range(SHIFTS):
                values = xs[j, pl.ds(pl.multiple_of(x_row + r, 8), chunk), :]
                w[pl.ds(r, chunk), pl.ds(j * tile, tile)] = ((values - mean) * scale).astype(
                    jnp.bfloat16
                )

    def multiply(step, w, part):
        first = lax.rem(step, groups) * SHIFTS + part * per_slice
        weights = jnp.concatenate([u_ref[0, first + j] for j in range(per_slice)], axis=1)
        depth = pl.ds(part * per_slice * tile, per_slice * tile)
        contract = (((1,), (1,)), ((), ()))
        left = lax.dot_general(
            w[pl.ds(0, half), depth], weights, contract, preferred_element_type=jnp.float32
        )
        right = lax.dot_general(
            weights, w[pl.ds(half, half), depth], contract, preferred_element_type=jnp.float32
        )
        return left, right

    def both(step, w, next_step, w_next):
        left, right = None, None
        for part in range(slices):
            if w is not None:
                more_left, more_right = multiply(step, w, part)
                left = more_left if left is None else left + more_left
                right = more_right if right is None else right + more_right
            if w_next is not None:
                build(next_step, w_next, part)
        if w is not None:
            block = step // groups
            first_row = pl.multiple_of(block * rows, rows)
            early[pl.ds(pl.multiple_of(block * half, half), half), :] += left
            out_ref[:, pl.ds(first_row + half, half)] += right

    both(None, None, jnp.int32(0), w_even)

    def pair(i, carry):
        both(2 * i, w_even, 2 * i + 1, w_odd)
        both(2 * i + 1, w_odd, 2 * i + 2, w_even)
        return carry

    pairs = (steps - 1) // 2
    lax.fori_loop(0, pairs, pair, 0)
    if 2 * pairs + 1 < steps:
        both(jnp.int32(2 * pairs), w_even, jnp.int32(steps - 1), w_odd)
        both(jnp.int32(steps - 1), w_odd, None, None)
    else:
        both(jnp.int32(2 * pairs), w_even, None, None)

    @pl.when(pl.program_id(0) == pl.num_programs(0) - 1)
    def _():
        for i in range(blocks):
            out_ref[:, pl.ds(i * rows, half)] = jnp.transpose(early[pl.ds(i * half, half), :])


def correlate(unit, trace, lag_count):
    tiles, samples, count, tile = unit.shape
    span = trace.shape[0]
    groups = samples // SHIFTS
    rows = math.gcd(lag_count, 512)
    reach = lag_count + samples - SHIFTS
    return pl.pallas_call(
        functools.partial(correlate_kernel, groups, lag_count // rows),
        grid=(tiles,),
        in_specs=[
            pl.BlockSpec((span, tile), lambda i: (0, i)),
            pl.BlockSpec((1, samples, count, tile), lambda i: (i, 0, 0, 0)),
        ],
        out_specs=pl.BlockSpec((count, lag_count), lambda i: (0, 0)),
        out_shape=jax.ShapeDtypeStruct((count, lag_count), jnp.float32),
        scratch_shapes=[
            pltpu.VMEM((SHIFTS, reach, tile), jnp.float32),
            pltpu.VMEM((lag_count, tile), jnp.float32),
            pltpu.VMEM((lag_count, tile), jnp.float32),
            pltpu.VMEM((rows, SHIFTS * tile), jnp.bfloat16),
            pltpu.VMEM((rows, SHIFTS * tile), jnp.bfloat16),
            pltpu.VMEM((lag_count // 2, count), jnp.float32),
        ],
        compiler_params=pltpu.CompilerParams(vmem_limit_bytes=VMEM_LIMIT),
        name="correlate_windows",
    )(trace, unit)


def sum_kernel(scale, part_ref, out_ref, outgoing, arrived, send_sem, recv_sem):
    n_chan, n_time = lax.axis_size("ch"), lax.axis_size("ta")
    chan, time = lax.axis_index("ch"), lax.axis_index("ta")
    owners = n_chan // n_time
    block, lags = out_ref.shape
    giver = chan // owners
    own = giver == time

    barrier = pltpu.get_barrier_semaphore()
    for i in range(n_chan):

        @pl.when(jnp.logical_not(own & (chan == i)))
        def _():
            pl.semaphore_signal(
                barrier, inc=1, device_id=(i, giver), device_id_type=pl.DeviceIdType.MESH
            )

    for r in range(owners):
        for b in range(n_time):
            outgoing[r * n_time + b] = part_ref[
                pl.ds(r * block, block), pl.ds(b * lags, lags)
            ]
    pl.semaphore_wait(barrier, owners * n_time - own.astype(jnp.int32))

    def copy(slot, r, b):
        return pltpu.make_async_remote_copy(
            src_ref=outgoing.at[slot],
            dst_ref=arrived.at[chan],
            send_sem=send_sem.at[slot],
            recv_sem=recv_sem.at[chan],
            device_id=(time * owners + r, b),
            device_id_type=pl.DeviceIdType.MESH,
        )

    for r in range(owners):
        for b in range(n_time):
            slot = r * n_time + b
            mine = (time * owners + r == chan) & (time == b)

            @pl.when(jnp.logical_not(mine))
            def _():
                copy(slot, r, b).start()

            @pl.when(mine)
            def _():
                arrived[chan] = outgoing[slot]

    for i in range(n_chan):

        @pl.when(jnp.logical_not(own & (chan == i)))
        def _():
            pltpu.make_async_remote_copy(
                src_ref=outgoing.at[0],
                dst_ref=arrived.at[i],
                send_sem=send_sem.at[0],
                recv_sem=recv_sem.at[i],
                device_id=(i, giver),
                device_id_type=pl.DeviceIdType.MESH,
            ).wait_recv()

    total = arrived[0]
    for i in range(1, n_chan):
        total = total + arrived[i]
    out_ref[...] = total * scale

    for r in range(owners):
        for b in range(n_time):
            mine = (time * owners + r == chan) & (time == b)

            @pl.when(jnp.logical_not(mine))
            def _():
                copy(r * n_time + b, r, b).wait_send()


def sum_to_owners(part, n_chan, n_time, scale):
    count, lag_count = part.shape
    owners = n_chan // n_time
    block, lags = count // owners, lag_count // n_time
    return pl.pallas_call(
        functools.partial(sum_kernel, scale),
        out_shape=jax.ShapeDtypeStruct((block, lags), jnp.float32),
        in_specs=[pl.BlockSpec(memory_space=pltpu.VMEM)],
        out_specs=pl.BlockSpec(memory_space=pltpu.VMEM),
        scratch_shapes=[
            pltpu.VMEM((owners * n_time, block, lags), jnp.float32),
            pltpu.VMEM((n_chan, block, lags), jnp.float32),
            pltpu.SemaphoreType.DMA((owners * n_time,)),
            pltpu.SemaphoreType.DMA((n_chan,)),
        ],
        compiler_params=pltpu.CompilerParams(
            collective_id=0, has_side_effects=True, vmem_limit_bytes=VMEM_LIMIT
        ),
        name="sum_to_owners",
    )(part)


def on_device(templates, record, record_tail):
    n_chan = lax.axis_size("ch")
    n_time = lax.axis_size("ta")
    tile = math.gcd(record.shape[0], 2 * LANES)
    unit, trace = prepare(templates, record, jnp.transpose(record_tail), n_time, tile)
    part = correlate(unit, trace, record.shape[1] * n_time)
    return sum_to_owners(part, n_chan, n_time, 1.0 / (n_chan * record.shape[0]))


def solution(mesh):
    return jax.shard_map(
        on_device,
        mesh=mesh,
        in_specs=(P("ta", None, "ch"), P("ch", "ta"), P("ch", None)),
        out_specs=P("ch", "ta"),
        check_vma=False,
    )
```

```python
import functools
import math

import jax
import jax.numpy as jnp
from jax import lax
from jax.experimental import pallas as pl
from jax.experimental.pallas import tpu as pltpu
from jax.sharding import PartitionSpec as P

LANES = 128
SHIFTS = 8
VMEM_LIMIT = 56 * 1024 * 1024


def prepare_kernel(last, t_ref, rec_ref, tail_ref, u_ref, trace_ref, wide, slabs, send_sem, recv_sem):
    n_time = lax.axis_size("ta")
    time = lax.axis_index("ta")
    rows, samples, _ = t_ref.shape
    lags = rec_ref.shape[1]
    stride = wide.shape[0] // samples
    step = (pl.program_id(0) * pl.num_programs(1) + pl.program_id(1)) * pl.num_programs(
        2
    ) + pl.program_id(2)

    def copy(i):
        return pltpu.make_async_remote_copy(
            src_ref=slabs.at[time],
            dst_ref=slabs.at[time],
            send_sem=send_sem.at[i - 1],
            recv_sem=recv_sem.at[i - 1],
            device_id={"ta": lax.rem(time + i, n_time)},
            device_id_type=pl.DeviceIdType.MESH,
        )

    @pl.when(step == 0)
    def _():
        barrier = pltpu.get_barrier_semaphore()
        for i in range(1, n_time):
            pl.semaphore_signal(
                barrier,
                inc=1,
                device_id={"ta": lax.rem(time + i, n_time)},
                device_id_type=pl.DeviceIdType.MESH,
            )
        slabs[time] = jnp.transpose(rec_ref[...])

    @pl.when(step == min(1, last))
    def _():
        pl.semaphore_wait(pltpu.get_barrier_semaphore(), n_time - 1)
        for i in range(1, n_time):
            copy(i).start()

    def one(k, carry):
        values = t_ref[k].astype(jnp.float32)
        centred = values - jnp.mean(values, axis=0, keepdims=True)
        power = jnp.mean(centred * centred, axis=0, keepdims=True)
        wide[pl.ds(k, samples, stride=stride), :] = centred * (
            lax.rsqrt(power + 1e-06) * (1.0 / math.sqrt(samples))
        )
        return carry

    lax.fori_loop(0, rows, one, 0, unroll=4)

    def cast(i, carry):
        first = i * SHIFTS
        part = wide[pl.ds(pl.multiple_of(first * stride, 8), SHIFTS * stride), :]
        part = part.reshape(SHIFTS, stride, LANES)[:, :rows]
        u_ref[0, pl.ds(first, SHIFTS)] = part.astype(jnp.bfloat16)
        return carry

    lax.fori_loop(0, samples // SHIFTS, cast, 0, unroll=5)

    @pl.when(step == last)
    def _():
        trace_ref[pl.ds(n_time * lags, tail_ref.shape[0]), :] = tail_ref[...]
        for i in range(1, n_time):
            copy(i).wait_recv()
        for i in range(n_time):
            trace_ref[pl.ds(i * lags, lags), :] = slabs[i]
        for i in range(1, n_time):
            copy(i).wait_send()


def prepare(templates, record, tail, n_time, tile):
    count, samples, channels = templates.shape
    lags = record.shape[1]
    span = n_time * lags + tail.shape[0]
    rows = math.gcd(count, 16)
    per_tile = tile // LANES
    grid = (channels // tile, per_tile, count // rows)
    return pl.pallas_call(
        functools.partial(prepare_kernel, math.prod(grid) - 1),
        grid=grid,
        in_specs=[
            pl.BlockSpec((rows, samples, LANES), lambda i, h, r: (r, 0, i * per_tile + h)),
            pl.BlockSpec(record.shape, lambda i, h, r: (0, 0)),
            pl.BlockSpec(tail.shape, lambda i, h, r: (0, 0)),
        ],
        out_specs=[
            pl.BlockSpec((1, samples, rows, LANES), lambda i, h, r: (i, 0, r, h)),
            pl.BlockSpec((span, channels), lambda i, h, r: (0, 0)),
        ],
        out_shape=[
            jax.ShapeDtypeStruct((channels // tile, samples, count, tile), jnp.bfloat16),
            jax.ShapeDtypeStruct((span, channels), jnp.float32),
        ],
        scratch_shapes=[
            pltpu.VMEM((samples * (rows + SHIFTS), LANES), jnp.float32),
            pltpu.VMEM((n_time, lags, channels), jnp.float32),
            pltpu.SemaphoreType.DMA((n_time - 1,)),
            pltpu.SemaphoreType.DMA((n_time - 1,)),
        ],
        compiler_params=pltpu.CompilerParams(
            collective_id=1, has_side_effects=True, vmem_limit_bytes=VMEM_LIMIT
        ),
        name="prepare",
    )(templates, record, tail)


def merge(left, right, n_left, n_right):
    (a0, v0), (a1, v1) = left, right
    w1 = n_right / (n_left + n_right)
    w0 = 1.0 - w1
    gap = a1 - a0
    return (a0 + w1 * gap, w0 * v0 + w1 * v1 + (w0 * w1) * (gap * gap))


def window_stats(xs, samples, lag_count):
    mean = xs[0]
    for j in range(1, SHIFTS):
        mean = mean + xs[j]
    mean = mean * (1.0 / SHIFTS)
    var = None
    for j in range(SHIFTS):
        gap = xs[j] - mean
        var = gap * gap if var is None else var + gap * gap
    var = var * (1.0 / SHIFTS)
    total, done, length = None, 0, SHIFTS
    while True:
        if samples & length:
            piece = (mean[done : done + lag_count], var[done : done + lag_count])
            total = piece if total is None else merge(total, piece, done, length)
            done += length
        if 2 * length > samples:
            return total
        keep = mean.shape[0] - length
        mean, var = merge(
            (mean[:keep], var[:keep]), (mean[length:], var[length:]), length, length
        )
        length *= 2


def correlate_kernel(groups, blocks, x_ref, u_ref, out_ref, xs, mu, rs, w_even, w_odd, early):
    rows = w_even.shape[0]
    tile = x_ref.shape[1]
    lag_count = mu.shape[0]
    samples = groups * SHIFTS
    reach = xs.shape[1]
    steps = groups * blocks

    @pl.when(pl.program_id(0) == 0)
    def _():
        out_ref[...] = jnp.zeros_like(out_ref)
        early[...] = jnp.zeros_like(early)

    x = x_ref[...]
    for j in range(SHIFTS):
        xs[j] = x[j : j + reach]
    mean, var = window_stats(xs, samples, lag_count)
    mu[...] = mean
    rs[...] = lax.rsqrt(var + 1e-06) * (1.0 / math.sqrt(samples))

    half = rows // 2
    chunk = math.gcd(rows, 32)
    slices = math.gcd(4, rows // chunk)
    per_slice = SHIFTS // slices

    def build(step, w, part):
        first_row = pl.multiple_of((step // groups) * rows, rows)
        x_row = first_row + lax.rem(step, groups) * SHIFTS
        for r in range(part * (rows // slices), (part + 1) * (rows // slices), chunk):
            mean = mu[pl.ds(first_row + r, chunk), :]
            scale = rs[pl.ds(first_row + r, chunk), :]
            for j in range(SHIFTS):
                values = xs[j, pl.ds(pl.multiple_of(x_row + r, 8), chunk), :]
                w[pl.ds(r, chunk), pl.ds(j * tile, tile)] = ((values - mean) * scale).astype(
                    jnp.bfloat16
                )

    def multiply(step, w, part):
        first = lax.rem(step, groups) * SHIFTS + part * per_slice
        weights = jnp.concatenate([u_ref[0, first + j] for j in range(per_slice)], axis=1)
        depth = pl.ds(part * per_slice * tile, per_slice * tile)
        contract = (((1,), (1,)), ((), ()))
        left = lax.dot_general(
            w[pl.ds(0, half), depth], weights, contract, preferred_element_type=jnp.float32
        )
        right = lax.dot_general(
            weights, w[pl.ds(half, half), depth], contract, preferred_element_type=jnp.float32
        )
        return left, right

    def both(step, w, next_step, w_next):
        left, right = None, None
        for part in range(slices):
            if w is not None:
                more_left, more_right = multiply(step, w, part)
                left = more_left if left is None else left + more_left
                right = more_right if right is None else right + more_right
            if w_next is not None:
                build(next_step, w_next, part)
        if w is not None:
            block = step // groups
            first_row = pl.multiple_of(block * rows, rows)
            early[pl.ds(pl.multiple_of(block * half, half), half), :] += left
            out_ref[:, pl.ds(first_row + half, half)] += right

    both(None, None, jnp.int32(0), w_even)

    def pair(i, carry):
        both(2 * i, w_even, 2 * i + 1, w_odd)
        both(2 * i + 1, w_odd, 2 * i + 2, w_even)
        return carry

    pairs = (steps - 1) // 2
    lax.fori_loop(0, pairs, pair, 0)
    if 2 * pairs + 1 < steps:
        both(jnp.int32(2 * pairs), w_even, jnp.int32(steps - 1), w_odd)
        both(jnp.int32(steps - 1), w_odd, None, None)
    else:
        both(jnp.int32(2 * pairs), w_even, None, None)

    @pl.when(pl.program_id(0) == pl.num_programs(0) - 1)
    def _():
        for i in range(blocks):
            out_ref[:, pl.ds(i * rows, half)] = jnp.transpose(early[pl.ds(i * half, half), :])


def correlate(unit, trace, lag_count):
    tiles, samples, count, tile = unit.shape
    span = trace.shape[0]
    groups = samples // SHIFTS
    rows = math.gcd(lag_count, 512)
    reach = lag_count + samples - SHIFTS
    return pl.pallas_call(
        functools.partial(correlate_kernel, groups, lag_count // rows),
        grid=(tiles,),
        in_specs=[
            pl.BlockSpec((span, tile), lambda i: (0, i)),
            pl.BlockSpec((1, samples, count, tile), lambda i: (i, 0, 0, 0)),
        ],
        out_specs=pl.BlockSpec((count, lag_count), lambda i: (0, 0)),
        out_shape=jax.ShapeDtypeStruct((count, lag_count), jnp.float32),
        scratch_shapes=[
            pltpu.VMEM((SHIFTS, reach, tile), jnp.float32),
            pltpu.VMEM((lag_count, tile), jnp.float32),
            pltpu.VMEM((lag_count, tile), jnp.float32),
            pltpu.VMEM((rows, SHIFTS * tile), jnp.bfloat16),
            pltpu.VMEM((rows, SHIFTS * tile), jnp.bfloat16),
            pltpu.VMEM((lag_count // 2, count), jnp.float32),
        ],
        compiler_params=pltpu.CompilerParams(vmem_limit_bytes=VMEM_LIMIT),
        name="correlate_windows",
    )(trace, unit)


def sum_kernel(scale, part_ref, out_ref, outgoing, arrived, send_sem, recv_sem):
    n_chan, n_time = lax.axis_size("ch"), lax.axis_size("ta")
    chan, time = lax.axis_index("ch"), lax.axis_index("ta")
    owners = n_chan // n_time
    block, lags = out_ref.shape
    giver = chan // owners
    own = giver == time

    barrier = pltpu.get_barrier_semaphore()
    for i in range(n_chan):

        @pl.when(jnp.logical_not(own & (chan == i)))
        def _():
            pl.semaphore_signal(
                barrier, inc=1, device_id=(i, giver), device_id_type=pl.DeviceIdType.MESH
            )

    for r in range(owners):
        for b in range(n_time):
            outgoing[r * n_time + b] = part_ref[
                pl.ds(r * block, block), pl.ds(b * lags, lags)
            ]
    pl.semaphore_wait(barrier, owners * n_time - own.astype(jnp.int32))

    def copy(slot, r, b):
        return pltpu.make_async_remote_copy(
            src_ref=outgoing.at[slot],
            dst_ref=arrived.at[chan],
            send_sem=send_sem.at[slot],
            recv_sem=recv_sem.at[chan],
            device_id=(time * owners + r, b),
            device_id_type=pl.DeviceIdType.MESH,
        )

    for r in range(owners):
        for b in range(n_time):
            slot = r * n_time + b
            mine = (time * owners + r == chan) & (time == b)

            @pl.when(jnp.logical_not(mine))
            def _():
                copy(slot, r, b).start()

            @pl.when(mine)
            def _():
                arrived[chan] = outgoing[slot]

    for i in range(n_chan):

        @pl.when(jnp.logical_not(own & (chan == i)))
        def _():
            pltpu.make_async_remote_copy(
                src_ref=outgoing.at[0],
                dst_ref=arrived.at[i],
                send_sem=send_sem.at[0],
                recv_sem=recv_sem.at[i],
                device_id=(i, giver),
                device_id_type=pl.DeviceIdType.MESH,
            ).wait_recv()

    total = arrived[0]
    for i in range(1, n_chan):
        total = total + arrived[i]
    out_ref[...] = total * scale

    for r in range(owners):
        for b in range(n_time):
            mine = (time * owners + r == chan) & (time == b)

            @pl.when(jnp.logical_not(mine))
            def _():
                copy(r * n_time + b, r, b).wait_send()


def sum_to_owners(part, n_chan, n_time, scale):
    count, lag_count = part.shape
    owners = n_chan // n_time
    block, lags = count // owners, lag_count // n_time
    return pl.pallas_call(
        functools.partial(sum_kernel, scale),
        out_shape=jax.ShapeDtypeStruct((block, lags), jnp.float32),
        in_specs=[pl.BlockSpec(memory_space=pltpu.VMEM)],
        out_specs=pl.BlockSpec(memory_space=pltpu.VMEM),
        scratch_shapes=[
            pltpu.VMEM((owners * n_time, block, lags), jnp.float32),
            pltpu.VMEM((n_chan, block, lags), jnp.float32),
            pltpu.SemaphoreType.DMA((owners * n_time,)),
            pltpu.SemaphoreType.DMA((n_chan,)),
        ],
        compiler_params=pltpu.CompilerParams(
            collective_id=0, has_side_effects=True, vmem_limit_bytes=VMEM_LIMIT
        ),
        name="sum_to_owners",
    )(part)


def on_device(templates, record, record_tail):
    n_chan = lax.axis_size("ch")
    n_time = lax.axis_size("ta")
    tile = math.gcd(record.shape[0], 2 * LANES)
    unit, trace = prepare(templates, record, jnp.transpose(record_tail), n_time, tile)
    part = correlate(unit, trace, record.shape[1] * n_time)
    return sum_to_owners(part, n_chan, n_time, 1.0 / (n_chan * record.shape[0]))


def solution(mesh):
    return jax.shard_map(
        on_device,
        mesh=mesh,
        in_specs=(P("ta", None, "ch"), P("ch", "ta"), P("ch", None)),
        out_specs=P("ch", "ta"),
        check_vma=False,
    )
```
